32 devices in a mesh: run: 2 (over x), gy: 16 (over z, y, core).
Axes of the slice: x: 2, y: 2, z: 4, core: 2. Of those that a mesh axis runs over, the one named last changes fastest.
Arguments:
- conserved: float32 [5, 16, 128, 128], P(None, 'run', 'gy'), parts along dimension 1, may hold values from -1.5 to 5, as said below
- target: float32 [3, 16, 128, 128], P(None, 'run', 'gy'), parts along dimension 1, may hold values from -2 to 2
Outputs:
- grad_state: float32 [5, 16, 128, 128], P(None, 'run', 'gy'), parts along dimension 1
- vorticity: float32 [3, 16, 128, 128], P(None, 'run', 'gy'), parts along dimension 1
The draws below stay inside these ranges and needn't reach their ends.
There are 2 independent parts, one for each index of `run`. The reference program is written for one: setup_inputs(seed, part) draws one part's arguments, and reference() takes and returns one part's arrays. A program takes and returns all parts, laid end to end along the dimension named above; each array names one. Nothing has to cross between parts.
Inputs may be any that keep to these rules, and one draw needn't show every extreme that they name: conserved[0] is the density, between 0.75 and 1.25; conserved[1:4] is density times a velocity of magnitude under 0.8 per component; conserved[4] is the total energy, with a pressure between 0.75 and 1.25.
All inputs are finite; a program needn't handle non-finite values.
Results may differ from the reference program's by a relative error of at most 0.00002.
Values sent between devices are 32-bit elements; how exact they have to be, the bound alone decides.
A program may use at most 64 MiB of HBM per device.

```python
import jax
import jax.numpy as jnp
from jax import lax

NX = 8
NZ = 128
NY = 128


def draw_state_fields(density_key, pressure_key, density_low, density_high, pressure_low, pressure_high):
    grid_shape = (NX, NY, NZ)
    density = jax.random.uniform(density_key, grid_shape, jnp.float32, density_low, density_high)
    pressure = jax.random.uniform(pressure_key, grid_shape, jnp.float32, pressure_low, pressure_high)
    return (density, pressure)


def draw_conserved(key, part):
    key = jax.random.fold_in(key, 11)
    density_key, motion_key, pressure_key = jax.random.split(key, 3)
    grid_shape = (NX, NY, NZ)
    density, pressure = draw_state_fields(density_key, pressure_key, 0.8, 1.2, 0.8, 1.2)
    motion = 0.3 * jax.random.truncated_normal(motion_key, -2.6, 2.6, (3,) + grid_shape, jnp.float32)
    momentum = density[None] * motion
    energy = pressure / 0.4 + 0.5 * density * jnp.sum(motion * motion, axis=0)
    return jnp.concatenate([density[None], momentum, energy[None]], axis=0).astype(jnp.float32)


def block_levels(stream_key, dims, cuts, least, top_value):
    def one(position, parts):
        heights = jax.random.uniform(jax.random.fold_in(jax.random.fold_in(stream_key, 6), position), (parts,), jnp.float32, least / len(cuts), top_value / len(cuts))
        return jnp.repeat(jnp.exp(heights), dims[position] // parts).reshape((-1,) + (1,) * (len(dims) - position - 1))

    loudness = one(*cuts[0])
    for cut in cuts[1:]:
        loudness = loudness * one(*cut)
    return loudness


def bell_draw(own_key, extent, spread, limit, cuts=(), held_as=jnp.bfloat16):
    values = spread * jax.random.normal(own_key, extent, jnp.float32)
    if cuts:
        values = values * block_levels(own_key, extent, cuts, -0.22, 0.18)
    return jnp.clip(values, -limit, limit).astype(held_as)


def setup_inputs(seed: int = 0, part: int = 0) -> dict:
    key_list = jax.random.split(jax.random.key(seed), 3)
    part_splits = jax.random.split(jax.random.fold_in(key_list[2], part), 3)
    conserved = draw_conserved(jax.random.fold_in(jax.random.fold_in(key_list[2], part), 71), part)
    target = bell_draw(part_splits[1], (3, NX, NY, NZ), 0.3, 2.0, ((2, 16),), jnp.float32)
    return dict(conserved=conserved, target=target)


GAMMA = 1.4
SPEED = 2.5
DT = 0.2
weno_eps = 0.1

def weno_face(far_left, near_left, centre, near_right, far_right):
    cand_low = (2.0 * far_left - 7.0 * near_left + 11.0 * centre) / 6.0
    cand_mid = (-near_left + 5.0 * centre + 2.0 * near_right) / 6.0
    cand_high = (2.0 * centre + 5.0 * near_right - far_right) / 6.0
    smooth_low = 13.0 / 12.0 * (far_left - 2.0 * near_left + centre) ** 2 + 0.25 * (far_left - 4.0 * near_left + 3.0 * centre) ** 2
    middle_smoothness_indicator = 13.0 / 12.0 * (near_left - 2.0 * centre + near_right) ** 2 + 0.25 * (near_left - near_right) ** 2
    smooth_high = 13.0 / 12.0 * (centre - 2.0 * near_right + far_right) ** 2 + 0.25 * (3.0 * centre - 4.0 * near_right + far_right) ** 2
    contrast = (smooth_low - smooth_high) ** 2
    weight_low = 0.1 * (1.0 + contrast / (smooth_low + weno_eps) ** 2)
    weight_mid = 0.6 * (1.0 + contrast / (middle_smoothness_indicator + weno_eps) ** 2)
    weight_high = 0.3 * (1.0 + contrast / (smooth_high + weno_eps) ** 2)
    return (weight_low * cand_low + weight_mid * cand_mid + weight_high * cand_high) / (weight_low + weight_mid + weight_high)

def split_fluxes(conserved, direction):
    density = conserved[0]
    momentum = conserved[1:4]
    energy = conserved[4]
    velocity = momentum / density
    pressure = (GAMMA - 1.0) * (energy - 0.5 * lax.optimization_barrier(jnp.sum(momentum * velocity, axis=0)))
    normal_speed = velocity[direction]
    pieces = [momentum[direction]]
    for component in range(3):
        product_term = momentum[component] * normal_speed
        if component == direction:
            product_term = product_term + pressure
        pieces.append(product_term)
    pieces.append((energy + pressure) * normal_speed)
    flux_rows = jnp.stack(pieces)
    return (0.5 * (flux_rows + SPEED * conserved), 0.5 * (flux_rows - SPEED * conserved))

def face_values(plus_part, negative_split_flux, offset):

    def single(members):
        upper_part, lower_part = members
        from_left = weno_face(offset(upper_part, -2), offset(upper_part, -1), offset(upper_part, 0), offset(upper_part, 1), offset(upper_part, 2))
        from_right = weno_face(offset(lower_part, 3), offset(lower_part, 2), offset(lower_part, 1), offset(lower_part, 0), offset(lower_part, -1))
        return from_left + from_right
    return lax.map(jax.checkpoint(single), (plus_part, negative_split_flux))

def periodic_term(conserved, direction):
    plus_part, negative_split_flux = split_fluxes(conserved, direction)

    def offset(values, shift_by):
        return jnp.roll(values, -shift_by, axis=direction)
    face_flux = face_values(plus_part, negative_split_flux, offset)
    return -(face_flux - jnp.roll(face_flux, 1, axis=direction + 1))

def rate_periodic(conserved):
    return periodic_term(conserved, 0) + periodic_term(conserved, 1) + periodic_term(conserved, 2)

def central(values, direction):
    return 0.5 * (jnp.roll(values, -1, axis=direction) - jnp.roll(values, 1, axis=direction))

def curl_periodic(velocity):
    return jnp.stack([central(velocity[2], 1) - central(velocity[1], 2), central(velocity[0], 2) - central(velocity[2], 0), central(velocity[1], 0) - central(velocity[0], 1)])

def forward(conserved):
    section_rate = jax.checkpoint(rate_periodic)
    section_one = conserved + DT * section_rate(conserved)
    section_two = 0.75 * conserved + 0.25 * (section_one + DT * section_rate(section_one))
    velocity = section_two[1:4] / section_two[0]
    return curl_periodic(velocity)

def reference(conserved, target):
    vorticity, pullback = jax.vjp(forward, conserved)
    grad_state, = pullback(vorticity - target)
    return (grad_state, vorticity)
```

```python
import functools

import jax
import jax.numpy as jnp
from jax import lax
from jax.experimental import pallas as pl
from jax.experimental.pallas import tpu as pltpu
from jax.sharding import PartitionSpec as P

SPEED = 2.5
DT = 0.2
X_AXIS, Z_AXIS = 0, 1
MESH = pl.DeviceIdType.MESH


def inv(x):
    return pltpu.reciprocal(x, approx=True)


def prv(x, axis):
    return pltpu.roll(x, 1, axis)


def nxt(x, axis):
    return pltpu.roll(x, x.shape[axis] - 1, axis)


def flow(u):
    ir = inv(u[0])
    v = [u[k] * ir for k in (1, 2, 3)]
    p = 0.4 * (u[4] - 0.5 * (u[1] * v[0] + u[2] * v[1] + u[3] * v[2]))
    return ir, v, p


def split(u, v, p, d):
    vd = v[d]
    flux = [u[d + 1]]
    for k in range(3):
        term = u[k + 1] * vd
        flux.append(term + p if k == d else term)
    flux.append((u[4] + p) * vd)
    out = []
    for f, q in zip(flux, u):
        half, wave = 0.5 * f, (0.5 * SPEED) * q
        out.append((half + wave, half - wave))
    return out


def split_adjoint(u, ir, v, p, d, gp, gm, grad):
    f = [None if a is None else 0.5 * (a + b) for a, b in zip(gp, gm)]
    for k in range(5):
        if gp[k] is not None:
            grad[k] = plus(grad[k], (0.5 * SPEED) * (gp[k] - gm[k]))
    vd = v[d]
    cp = f[d + 1]
    cv = f[1] * u[1] + f[2] * u[2] + f[3] * u[3]
    if f[4] is not None:
        cp = cp + f[4] * vd
        cv = cv + f[4] * (u[4] + p)
        grad[4] = plus(grad[4], f[4] * vd)
    cp = 0.4 * cp
    grad[4] = plus(grad[4], cp)
    cv = cv * ir
    for k in range(3):
        grad[k + 1] = plus(grad[k + 1], f[k + 1] * vd - v[k] * cp)
    grad[d + 1] = grad[d + 1] + (f[0] + cv)
    speed2 = v[0] * v[0] + v[1] * v[1] + v[2] * v[2]
    grad[0] = plus(grad[0], 0.5 * speed2 * cp - cv * vd)


def plus(a, b):
    return b if a is None else a + b


def cell(um, u, up):
    m = up - um
    d = (up - u) - (u - um)
    e = d + d
    q = (13.0 / 3.0) * (d * d) + 0.4
    a, b = m + e, m - e
    return m, d, q + m * m, q + a * a, q + b * b


LINEAR = ((1.0, 3.0), (3.0, 1.0))
SLOPE = ((1.0 / 3.0, 0.5), (0.5, 1.0 / 3.0))


def correction(bm, bc, bp, tm, tp, side):
    lm, lp = LINEAR[side]
    km, kp = SLOPE[side]
    tau = bm - bp
    ym, yc, yp = tau * inv(bm), tau * inv(bc), tau * inv(bp)
    zm, zc, zp = ym * ym, yc * yc, yp * yp
    total = (10.0 + lm * zm) + (6.0 * zc + lp * zp)
    top = (1.0 + zm) * (km * tm) + (1.0 + zp) * (kp * tp)
    return top * inv(total)


def correction_adjoint(h4, bm, bc, bp, tm, tp, side):
    lm, lp = LINEAR[side]
    km, kp = SLOPE[side]
    tau = bm - bp
    rm, rc, rp = inv(bm), inv(bc), inv(bp)
    ym, yc, yp = tau * rm, tau * rc, tau * rp
    zm, zc, zp = ym * ym, yc * yc, yp * yp
    am, ap = 1.0 + zm, 1.0 + zp
    ktm, ktp = km * tm, kp * tp
    rt = inv((10.0 + lm * zm) + (6.0 * zc + lp * zp))
    value = (am * ktm + ap * ktp) * rt
    gs = h4 * rt if side == 0 else -(h4 * rt)
    gv = gs * value
    dm = (gs * ktm - lm * gv) * (ym * rm)
    dc = (-6.0 * gv) * (yc * rc)
    dp = (gs * ktp - lp * gv) * (yp * rp)
    sk = dm + dc + dp
    return sk - dm * ym, -(dc * yc), -(sk + dp * yp), (0.25 * km) * (gs * am), (0.25 * kp) * (gs * ap)


def cell_adjoint(m, d, gc, gr, gl, d_extra, m_extra):
    both = gr + gl
    total = both + gc
    delta = 2.0 * (gr - gl)
    gm = total * m + delta * d + m_extra
    gd = ((13.0 / 3.0) * total + 4.0 * both) * d + delta * m + d_extra
    return gm, gd


def rolled_term(f, axis, side):
    m, d, bc, br, bl = cell(prv(f, axis), f, nxt(f, axis))
    tp = nxt(d, axis) - d
    r = correction(prv(br, axis), bc, nxt(bl, axis), prv(tp, axis), tp, side)
    if side == 0:
        a = (1.0 / 6.0) * d + r
        return a - prv(a, axis) - 0.5 * m
    a = (1.0 / 6.0) * d - r
    return nxt(a, axis) - a - 0.5 * m


def rolled_adjoint(f, lam, h4, axis, side):
    m, d, bc, br, bl = cell(prv(f, axis), f, nxt(f, axis))
    tp = nxt(d, axis) - d
    gbm, gbc, gbp, ctm, ctp = correction_adjoint(
        h4, prv(br, axis), bc, nxt(bl, axis), prv(tp, axis), tp, side
    )
    w = ctp + nxt(ctm, axis)
    extra = (1.0 / 24.0) * h4 + (prv(w, axis) - w)
    gm, gd = cell_adjoint(m, d, gbc, nxt(gbm, axis), prv(gbp, axis), extra, -0.5 * lam)
    return prv(gd + gm, axis) + nxt(gd - gm, axis) - 2.0 * gd


def central(x, axis):
    return 0.5 * (nxt(x, axis) - prv(x, axis))


def kernel(
    rows, c_ref, t_ref, g_ref, o_ref,
    u1, u2, wv, tg, res, rate, two, lam, f1, f2, yc1, yc2, za, gb, pq, gu1, gu2, rg1, rg2,
    send, recv,
):
    size = lax.axis_size("gy")
    me = lax.axis_index("gy")
    right, left = lax.rem(me + 1, size), lax.rem(me + size - 1, size)
    barrier = pltpu.get_barrier_semaphore()
    for other in (left, right):
        pl.semaphore_signal(barrier, inc=1, device_id={"gy": other}, device_id_type=MESH)

    def loop(low, high, body):
        lax.fori_loop(low, high, lambda i, _: (body(i), 0)[1], 0)

    def exchange(slot, pairs):
        copies = []
        for side, (other, (src, dst)) in enumerate(zip((left, right), pairs)):
            copies.append(
                pltpu.make_async_remote_copy(
                    src_ref=src, dst_ref=dst,
                    send_sem=send.at[slot, side], recv_sem=recv.at[slot, side],
                    device_id={"gy": other}, device_id_type=MESH,
                )
            )
        for copy in copies:
            copy.start()
        return copies

    def halo(slot, ref, width):
        return exchange(
            slot,
            (
                (ref.at[:, pl.ds(width, width)], ref.at[:, pl.ds(width + rows, width)]),
                (ref.at[:, pl.ds(rows, width)], ref.at[:, pl.ds(0, width)]),
            ),
        )

    def arrived(copies):
        for copy in copies:
            copy.wait_recv()

    def strided(component, row):
        return pl.ds(component * (8 * rows) + row, 8, stride=rows)

    def load_row(i):
        for c in range(5):
            u1[c, i + 3] = c_ref[strided(c, i), :]
        for c in range(3):
            tg[c, i + 1] = t_ref[strided(c, i), :]

    zero = jnp.zeros((8, 128), jnp.float32)

    loop(0, rows, load_row)
    pl.semaphore_wait(barrier, 2)
    copies_u = halo(0, u1, 3)
    copies_t = halo(1, tg, 1)

    def clear(i):
        for side in range(2):
            for c in range(5):
                for q in range(5):
                    gb[side, c, q, i] = zero
                    gb[side, c, q, i + rows + 3] = zero

    loop(0, 2, clear)

    def clear_pq(i):
        for side in range(2):
            for c in range(5):
                for q in range(3):
                    pq[side, c, q, i] = zero
                    pq[side, c, q, i + rows + 4] = zero

    loop(0, 4, clear_pq)

    def clear_lam(i):
        for c in range(5):
            lam[c, i] = zero
            lam[c, i + rows + 3] = zero

    loop(0, 3, clear_lam)

    def state(ref, row):
        return [ref[c, row] for c in range(5)]

    def flux_y(u_ref, f_ref, row):
        u = state(u_ref, row)
        _, v, p = flow(u)
        for c, pair in enumerate(split(u, v, p, 1)):
            f_ref[0, c, row] = pair[0]
            f_ref[1, c, row] = pair[1]

    def rate_local(u_ref, f_ref):
        def body(i):
            u = state(u_ref, i + 3)
            _, v, p = flow(u)
            for c, pair in enumerate(split(u, v, p, 1)):
                f_ref[0, c, i + 3] = pair[0]
                f_ref[1, c, i + 3] = pair[1]
            fx = split(u, v, p, 0)
            fz = split(u, v, p, 2)
            for c in range(5):
                total = None
                for side in range(2):
                    total = plus(total, rolled_term(fx[c][side], X_AXIS, side))
                    total = plus(total, rolled_term(fz[c][side], Z_AXIS, side))
                rate[c, i] = total

        loop(0, rows, body)

    def rate_y(u_ref, f_ref, yc):
        def edges(i):
            flux_y(u_ref, f_ref, i)
            flux_y(u_ref, f_ref, i + rows + 3)

        loop(0, 3, edges)

        def cells(i):
            for c in range(5):
                for side in range(2):
                    r = i + 1
                    values = cell(f_ref[side, c, r - 1], f_ref[side, c, r], f_ref[side, c, r + 1])
                    for q in range(5):
                        yc[side, c, q, r] = values[q]

        loop(0, rows + 4, cells)

        def faces(k):
            for c in range(5):
                total = None
                for side in range(2):
                    r = k + 2 + side
                    d = yc[side, c, 1, r]
                    x = correction(
                        yc[side, c, 3, r - 1], yc[side, c, 2, r], yc[side, c, 4, r + 1],
                        d - yc[side, c, 1, r - 1], yc[side, c, 1, r + 1] - d, side,
                    )
                    a = (1.0 / 6.0) * d
                    total = plus(total, a + x if side == 0 else a - x)
                za[c, k] = total

        loop(0, rows + 1, faces)

    def whole_rate(yc, c, i):
        return rate[c, i] + (
            (za[c, i + 1] - za[c, i]) - 0.5 * (yc[0, c, 0, i + 3] + yc[1, c, 0, i + 3])
        )

    rate_local(u1, f1)
    arrived(copies_u)
    rate_y(u1, f1, yc1)

    def first(i):
        for c in range(5):
            u2[c, i + 3] = u1[c, i + 3] + DT * whole_rate(yc1, c, i)

    loop(0, rows, first)
    copies_2 = halo(2, u2, 3)

    rate_local(u2, f2)
    arrived(copies_2)
    rate_y(u2, f2, yc2)

    def second(i):
        s = []
        for c in range(4):
            s.append(
                0.75 * u1[c, i + 3] + 0.25 * (u2[c, i + 3] + DT * whole_rate(yc2, c, i))
            )
        ir = inv(s[0])
        two[3, i] = ir
        for k in range(3):
            wv[k, i + 2] = s[k + 1] * ir

    loop(0, rows, second)
    copies_w = halo(3, wv, 2)
    arrived(copies_t)
    arrived(copies_w)

    def curl(i):
        x, y, z = wv[0, i + 1], wv[1, i + 1], wv[2, i + 1]
        vort = (
            0.5 * (wv[2, i + 2] - wv[2, i]) - central(y, Z_AXIS),
            central(x, Z_AXIS) - central(z, X_AXIS),
            central(y, X_AXIS) - 0.5 * (wv[0, i + 2] - wv[0, i]),
        )
        for k in range(3):
            res[k, i] = vort[k] - tg[k, i]
        return vort

    def curl_own(i):
        vort = curl(i + 1)
        for k in range(3):
            o_ref[strided(k, i), :] = vort[k]

    loop(0, rows, curl_own)
    curl(0)
    curl(rows + 1)

    def back_two(i):
        a, b, c = res[0, i + 1], res[1, i + 1], res[2, i + 1]
        gw = (
            0.5 * (res[2, i + 2] - res[2, i]) - central(b, Z_AXIS),
            central(a, Z_AXIS) - central(c, X_AXIS),
            central(b, X_AXIS) - 0.5 * (res[0, i + 2] - res[0, i]),
        )
        ir = two[3, i]
        gw = [ir * g for g in gw]
        grad = [-(gw[0] * wv[0, i + 2] + gw[1] * wv[1, i + 2] + gw[2] * wv[2, i + 2])] + gw
        for c in range(4):
            two[c, i] = grad[c]
            lam[c, i + 3] = (0.25 * DT) * grad[c]

    loop(0, rows, back_two)

    def back_y(slot, u_ref, yc, gu, rg, count):
        def faces(k):
            for c in range(count):
                h4 = 4.0 * (lam[c, k + 2] - lam[c, k + 3])
                for side in range(2):
                    r = k + 2 + side
                    d = yc[side, c, 1, r]
                    gbm, gbc, gbp, ctm, ctp = correction_adjoint(
                        h4, yc[side, c, 3, r - 1], yc[side, c, 2, r], yc[side, c, 4, r + 1],
                        d - yc[side, c, 1, r - 1], yc[side, c, 1, r + 1] - d, side,
                    )
                    centre = (ctm - ctp) + (1.0 / 24.0) * h4
                    for q, value in enumerate((gbm, gbc, gbp, ctm, ctp)):
                        gb[side, c, q, k + 2] = value
                    pq[side, c, 2, r + 1] = centre

        loop(0, rows + 1, faces)

        def cells(j):
            for c in range(count):
                for side in range(2):
                    r = j + 1 + side
                    extra = pq[side, c, 2, r + 1] + (gb[side, c, 4, j] - gb[side, c, 3, j + 2])
                    gm, gd = cell_adjoint(
                        yc[side, c, 0, r], yc[side, c, 1, r],
                        gb[side, c, 1, j + 1], gb[side, c, 0, j + 2], gb[side, c, 2, j],
                        extra, -0.5 * lam[c, r],
                    )
                    pq[side, c, 0, r + 1] = gd + gm
                    pq[side, c, 1, r + 1] = gd - gm

        loop(0, rows + 3, cells)

        def gather(r):
            u = state(u_ref, r)
            ir, v, p = flow(u)
            parts = ([None] * 5, [None] * 5)
            for c in range(count):
                for side in range(2):
                    parts[side][c] = (
                        pq[side, c, 0, r] + pq[side, c, 1, r + 2]
                        - (pq[side, c, 0, r + 1] + pq[side, c, 1, r + 1])
                    )
            grad = [None] * 5
            split_adjoint(u, ir, v, p, 1, parts[0], parts[1], grad)
            for c in range(5):
                gu[c, r] = grad[c]

        loop(0, rows + 6, gather)
        return exchange(
            slot,
            (
                (gu.at[:, pl.ds(0, 3)], rg.at[1]),
                (gu.at[:, pl.ds(rows + 3, 3)], rg.at[0]),
            ),
        )

    def back_local(u_ref, gu, count):
        def body(i):
            u = state(u_ref, i + 3)
            ir, v, p = flow(u)
            grad = [gu[c, i + 3] for c in range(5)]
            for d, axis in ((0, X_AXIS), (2, Z_AXIS)):
                f = split(u, v, p, d)
                parts = ([None] * 5, [None] * 5)
                for c in range(count):
                    value = lam[c, i + 3]
                    h4 = 4.0 * (value - nxt(value, axis))
                    parts[0][c] = rolled_adjoint(f[c][0], value, h4, axis, 0)
                    parts[1][c] = rolled_adjoint(f[c][1], value, prv(h4, axis), axis, 1)
                split_adjoint(u, ir, v, p, d, parts[0], parts[1], grad)
            for c in range(5):
                rate[c, i] = grad[c]

        loop(0, rows, body)

    def add_edges(rg):
        def body(i):
            for c in range(5):
                rate[c, i] = rate[c, i] + rg[0, c, i]

        def body_last(i):
            for c in range(5):
                rate[c, i + rows - 3] = rate[c, i + rows - 3] + rg[1, c, i]

        loop(0, 3, body)
        loop(0, 3, body_last)

    copies_g2 = back_y(4, u2, yc2, gu2, rg2, 4)
    back_local(u2, gu2, 4)
    arrived(copies_g2)
    add_edges(rg2)

    def grad_one(i):
        for c in range(5):
            value = rate[c, i] if c == 4 else 0.25 * two[c, i] + rate[c, i]
            lam[c, i + 3] = DT * value
            two[c, i] = value if c == 4 else 0.75 * two[c, i] + value

    loop(0, rows, grad_one)

    copies_g1 = back_y(5, u1, yc1, gu1, rg1, 5)
    back_local(u1, gu1, 5)
    arrived(copies_g1)
    add_edges(rg1)

    def finish(i):
        for c in range(5):
            g_ref[strided(c, i), :] = two[c, i] + rate[c, i]

    loop(0, rows, finish)
    for copies in (copies_u, copies_t, copies_2, copies_w, copies_g2, copies_g1):
        for copy in copies:
            copy.wait_send()


def body(conserved, target):
    rows = conserved.shape[2]
    tile = conserved.shape[1::2]

    def vmem(*lead):
        return pltpu.VMEM(lead + tile, jnp.float32)

    grad, vorticity = pl.pallas_call(
        functools.partial(kernel, rows),
        out_shape=(
            jax.ShapeDtypeStruct((5 * tile[0] * rows, tile[1]), jnp.float32),
            jax.ShapeDtypeStruct((3 * tile[0] * rows, tile[1]), jnp.float32),
        ),
        in_specs=[pl.BlockSpec(memory_space=pltpu.VMEM)] * 2,
        out_specs=[pl.BlockSpec(memory_space=pltpu.VMEM)] * 2,
        scratch_shapes=[
            vmem(5, rows + 6), vmem(5, rows + 6), vmem(3, rows + 4), vmem(3, rows + 2),
            vmem(3, rows + 2), vmem(5, rows), vmem(5, rows), vmem(5, rows + 6),
            vmem(2, 5, rows + 6), vmem(2, 5, rows + 6),
            vmem(2, 5, 5, rows + 6), vmem(2, 5, 5, rows + 6),
            vmem(5, rows + 1), vmem(2, 5, 5, rows + 5), vmem(2, 5, 3, rows + 8),
            vmem(5, rows + 6), vmem(5, rows + 6), vmem(2, 5, 3), vmem(2, 5, 3),
            pltpu.SemaphoreType.DMA((6, 2)),
            pltpu.SemaphoreType.DMA((6, 2)),
        ],
        compiler_params=pltpu.CompilerParams(
            collective_id=0, has_side_effects=True, vmem_limit_bytes=40 * 1024 * 1024
        ),
    )(conserved.reshape(-1, tile[1]), target.reshape(-1, tile[1]))
    return grad.reshape(conserved.shape), vorticity.reshape(target.shape)


def solution(mesh):
    spec = P(None, "run", "gy", None)
    return jax.shard_map(
        body, mesh=mesh, in_specs=(spec, spec), out_specs=(spec, spec), check_vma=False
    )
```

```python
import functools

import jax
import jax.numpy as jnp
from jax import lax
from jax.experimental import pallas as pl
from jax.experimental.pallas import tpu as pltpu
from jax.sharding import PartitionSpec as P

SPEED = 2.5
DT = 0.2
X_AXIS, Z_AXIS = 0, 1
MESH = pl.DeviceIdType.MESH


def inv(x):
    return pltpu.reciprocal(x, approx=True)


def prv(x, axis):
    return pltpu.roll(x, 1, axis)


def nxt(x, axis):
    return pltpu.roll(x, x.shape[axis] - 1, axis)


def flow(u):
    ir = inv(u[0])
    v = [u[k] * ir for k in (1, 2, 3)]
    p = 0.4 * (u[4] - 0.5 * (u[1] * v[0] + u[2] * v[1] + u[3] * v[2]))
    return ir, v, p


def split(u, v, p, d):
    vd = v[d]
    flux = [u[d + 1]]
    for k in range(3):
        term = u[k + 1] * vd
        flux.append(term + p if k == d else term)
    flux.append((u[4] + p) * vd)
    out = []
    for f, q in zip(flux, u):
        half, wave = 0.5 * f, (0.5 * SPEED) * q
        out.append((half + wave, half - wave))
    return out


def split_adjoint(u, ir, v, p, d, gp, gm, grad):
    f = [None if a is None else 0.5 * (a + b) for a, b in zip(gp, gm)]
    for k in range(5):
        if gp[k] is not None:
            grad[k] = plus(grad[k], (0.5 * SPEED) * (gp[k] - gm[k]))
    vd = v[d]
    cp = f[d + 1]
    cv = f[1] * u[1] + f[2] * u[2] + f[3] * u[3]
    if f[4] is not None:
        cp = cp + f[4] * vd
        cv = cv + f[4] * (u[4] + p)
        grad[4] = plus(grad[4], f[4] * vd)
    cp = 0.4 * cp
    grad[4] = plus(grad[4], cp)
    cv = cv * ir
    for k in range(3):
        grad[k + 1] = plus(grad[k + 1], f[k + 1] * vd - v[k] * cp)
    grad[d + 1] = grad[d + 1] + (f[0] + cv)
    speed2 = v[0] * v[0] + v[1] * v[1] + v[2] * v[2]
    grad[0] = plus(grad[0], 0.5 * speed2 * cp - cv * vd)


def plus(a, b):
    return b if a is None else a + b


def cell(um, u, up):
    m = up - um
    d = (up - u) - (u - um)
    e = d + d
    q = (13.0 / 3.0) * (d * d) + 0.4
    a, b = m + e, m - e
    return m, d, q + m * m, q + a * a, q + b * b


LINEAR = ((1.0, 3.0), (3.0, 1.0))
SLOPE = ((1.0 / 3.0, 0.5), (0.5, 1.0 / 3.0))


def correction(bm, bc, bp, tm, tp, side):
    lm, lp = LINEAR[side]
    km, kp = SLOPE[side]
    tau = bm - bp
    rm, rc, rp = inv(bm), inv(bc), inv(bp)
    ym, yc, yp = tau * rm, tau * rc, tau * rp
    zm, zc, zp = ym * ym, yc * yc, yp * yp
    am, ap = 1.0 + zm, 1.0 + zp
    ktm, ktp = km * tm, kp * tp
    rt = inv((10.0 + lm * zm) + (6.0 * zc + lp * zp))
    value = (am * ktm + ap * ktp) * rt
    if side == 1:
        rt = -rt
    dm = (ktm - lm * value) * (ym * rm)
    dc = (-6.0 * value) * (yc * rc)
    dp = (ktp - lp * value) * (yp * rp)
    sk = dm + dc + dp
    return value, (
        rt * (sk - dm * ym), rt * (-dc * yc), rt * (-sk - dp * yp), ((0.25 * km) * rt) * am, ((0.25 * kp) * rt) * ap
    )


def cell_adjoint(m, d, gc, gr, gl, d_extra, m_extra):
    both = gr + gl
    total = both + gc
    delta = 2.0 * (gr - gl)
    gm = total * m + delta * d + m_extra
    gd = ((13.0 / 3.0) * total + 4.0 * both) * d + delta * m + d_extra
    return gm, gd


def rolled_term(f, axis, side, keep):
    m, d, bc, br, bl = cell(prv(f, axis), f, nxt(f, axis))
    tp = nxt(d, axis) - d
    r, coefs = correction(prv(br, axis), bc, nxt(bl, axis), prv(tp, axis), tp, side)
    if keep is not None:
        keep((m, d) + coefs)
    if side == 0:
        a = (1.0 / 6.0) * d + r
        return a - prv(a, axis) - 0.5 * m
    a = (1.0 / 6.0) * d - r
    return nxt(a, axis) - a - 0.5 * m


def rolled_adjoint(kept, lam, h4, axis):
    m, d, cbm, cbc, cbp, ctm, ctp = kept
    w = h4 * ctp + nxt(h4 * ctm, axis)
    extra = (1.0 / 24.0) * h4 + (prv(w, axis) - w)
    gm, gd = cell_adjoint(
        m, d, h4 * cbc, nxt(h4 * cbm, axis), prv(h4 * cbp, axis), extra, -0.5 * lam
    )
    return prv(gd + gm, axis) + nxt(gd - gm, axis) - 2.0 * gd


def central(x, axis):
    return 0.5 * (nxt(x, axis) - prv(x, axis))


def kernel(
    rows, c_any, t_any, g_ref, o_ref,
    c_ref, t_ref, u1, u2, wv, tg, res, rate, two, ivs, lam, f1, f2, yc1, yc2, za, ys1, ys2,
    st1, st2, pq, gu1, gu2, rg1, rg2, local, send, recv,
):
    loads = [
        pltpu.make_async_copy(c_any, c_ref, local.at[0]),
        pltpu.make_async_copy(t_any, t_ref, local.at[1]),
    ]
    for load in loads:
        load.start()
    size = lax.axis_size("gy")
    me = lax.axis_index("gy")
    right, left = lax.rem(me + 1, size), lax.rem(me + size - 1, size)
    barrier = pltpu.get_barrier_semaphore()
    for other in (left, right):
        pl.semaphore_signal(barrier, inc=1, device_id={"gy": other}, device_id_type=MESH)

    def loop(low, high, body):
        lax.fori_loop(low, high, lambda i, _: (body(i), 0)[1], 0)

    def exchange(slot, pairs):
        copies = []
        for side, (other, (src, dst)) in enumerate(zip((left, right), pairs)):
            copies.append(
                pltpu.make_async_remote_copy(
                    src_ref=src, dst_ref=dst,
                    send_sem=send.at[slot, side], recv_sem=recv.at[slot, side],
                    device_id={"gy": other}, device_id_type=MESH,
                )
            )
        for copy in copies:
            copy.start()
        return copies

    def halo(slot, ref, width):
        return exchange(
            slot,
            (
                (ref.at[:, pl.ds(width, width)], ref.at[:, pl.ds(width + rows, width)]),
                (ref.at[:, pl.ds(rows, width)], ref.at[:, pl.ds(0, width)]),
            ),
        )

    def arrived(copies):
        for copy in copies:
            copy.wait_recv()

    def strided(component, row):
        return pl.ds(component * (8 * rows) + row, 8, stride=rows)

    def load_row(i):
        for c in range(5):
            u1[c, i + 3] = c_ref[strided(c, i), :]
        for c in range(3):
            tg[c, i + 1] = t_ref[strided(c, i), :]

    zero = jnp.zeros((8, 128), jnp.float32)

    for load in loads:
        load.wait()
    loop(0, rows, load_row)
    pl.semaphore_wait(barrier, 2)
    copies_u = halo(0, u1, 3)
    copies_t = halo(1, tg, 1)

    def clear(i):
        for side in range(2):
            for c in range(5):
                for q in range(5):
                    ys1[side, c, q, i] = zero
                    ys1[side, c, q, i + rows + 3] = zero

    loop(0, 2, clear)

    def clear_pq(i):
        for side in range(2):
            for c in range(5):
                for q in range(2):
                    pq[side, c, q, i] = zero
                    pq[side, c, q, i + rows + 5] = zero

    loop(0, 3, clear_pq)

    def clear_lam(i):
        for c in range(5):
            lam[c, i] = zero
            lam[c, i + rows + 3] = zero

    loop(0, 3, clear_lam)

    def state(ref, row):
        return [ref[c, row] for c in range(5)]

    def flux_y(u_ref, f_ref, row):
        u = state(u_ref, row)
        _, v, p = flow(u)
        for c, pair in enumerate(split(u, v, p, 1)):
            f_ref[0, c, row] = pair[0]
            f_ref[1, c, row] = pair[1]

    def row_rate(u_ref, f_ref, st, pad, count, i):
        u = state(u_ref, i + pad)
        _, v, p = flow(u)
        if st is not None:
            for c, pair in enumerate(split(u, v, p, 1)):
                f_ref[0, c, i + pad] = pair[0]
                f_ref[1, c, i + pad] = pair[1]
        fx = split(u, v, p, 0)
        fz = split(u, v, p, 2)
        for c in range(5):
            total = None
            for side in range(2):
                for number, f, axis in ((0, fx, X_AXIS), (1, fz, Z_AXIS)):

                    def keep(values):
                        for q, value in enumerate(values):
                            st[number, side, c, q, i] = value

                    use = keep if st is not None and c < count else None
                    total = plus(total, rolled_term(f[c][side], axis, side, use))
            rate[c, i + pad - 3] = total

    def rate_y(u_ref, f_ref, yc, ys, pad, count):
        extra = pad - 3

        def edges(i):
            flux_y(u_ref, f_ref, i)
            flux_y(u_ref, f_ref, i + rows + pad)

        loop(0, pad, edges)

        def cells(i):
            for c in range(5):
                for side in range(2):
                    r = i + 1
                    values = cell(f_ref[side, c, r - 1], f_ref[side, c, r], f_ref[side, c, r + 1])
                    for q in range(5):
                        yc[side, c, q, r] = values[q]

        loop(0, rows + 2 * pad - 2, cells)

        def faces(k):
            for c in range(5):
                total = None
                for side in range(2):
                    r = k + 2 + side
                    d = yc[side, c, 1, r]
                    x, coefs = correction(
                        yc[side, c, 3, r - 1], yc[side, c, 2, r], yc[side, c, 4, r + 1],
                        d - yc[side, c, 1, r - 1], yc[side, c, 1, r + 1] - d, side,
                    )
                    if c < count:
                        for q, value in enumerate(coefs):
                            ys[side, c, q, k + 2 - extra] = value
                    a = (1.0 / 6.0) * d
                    total = plus(total, a + x if side == 0 else a - x)
                za[c, k] = total

        loop(0, rows + 1 + 2 * extra, faces)

    def whole_rate(yc, c, i):
        return rate[c, i] + (
            (za[c, i + 1] - za[c, i]) - 0.5 * (yc[0, c, 0, i + 3] + yc[1, c, 0, i + 3])
        )

    loop(0, rows, lambda i: row_rate(u1, f1, st1, 3, 5, i))
    arrived(copies_u)
    rate_y(u1, f1, yc1, ys1, 3, 5)

    def first(i):
        for c in range(5):
            u2[c, i + 5] = u1[c, i + 3] + DT * whole_rate(yc1, c, i)

    loop(0, rows, first)
    copies_2 = halo(2, u2, 5)

    loop(0, rows, lambda i: row_rate(u2, f2, st2, 5, 4, i))
    arrived(copies_2)

    def beside(i):
        row_rate(u2, f2, None, 5, 4, i - 2)
        row_rate(u2, f2, None, 5, 4, i + rows)

    loop(0, 2, beside)
    rate_y(u2, f2, yc2, ys2, 5, 4)

    def second(i):
        s = []
        for c in range(4):
            s.append(
                0.75 * u1[c, i + 1] + 0.25 * (u2[c, i + 3] + DT * whole_rate(yc2, c, i))
            )
        ir = inv(s[0])
        ivs[i] = ir
        for k in range(3):
            wv[k, i] = s[k + 1] * ir

    loop(0, rows + 4, second)
    arrived(copies_t)

    def curl(i):
        x, y, z = wv[0, i + 1], wv[1, i + 1], wv[2, i + 1]
        vort = (
            0.5 * (wv[2, i + 2] - wv[2, i]) - central(y, Z_AXIS),
            central(x, Z_AXIS) - central(z, X_AXIS),
            central(y, X_AXIS) - 0.5 * (wv[0, i + 2] - wv[0, i]),
        )
        for k in range(3):
            res[k, i] = vort[k] - tg[k, i]
        return vort

    def curl_own(i):
        vort = curl(i + 1)
        for k in range(3):
            o_ref[strided(k, i), :] = vort[k]

    loop(0, rows, curl_own)
    curl(0)
    curl(rows + 1)

    def back_two(i):
        a, b, c = res[0, i + 1], res[1, i + 1], res[2, i + 1]
        gw = (
            0.5 * (res[2, i + 2] - res[2, i]) - central(b, Z_AXIS),
            central(a, Z_AXIS) - central(c, X_AXIS),
            central(b, X_AXIS) - 0.5 * (res[0, i + 2] - res[0, i]),
        )
        ir = ivs[i + 2]
        gw = [ir * g for g in gw]
        grad = [-(gw[0] * wv[0, i + 2] + gw[1] * wv[1, i + 2] + gw[2] * wv[2, i + 2])] + gw
        for c in range(4):
            two[c, i] = grad[c]
            lam[c, i + 3] = (0.25 * DT) * grad[c]

    loop(0, rows, back_two)

    def back_y(slot, u_ref, yc, ys, gu, rg, pad, count):
        extra = pad - 3

        def cells(j):
            for c in range(count):
                l0, l1, l2, l3 = (lam[c, j + n] for n in range(4))
                before, here, after = 4.0 * (l0 - l1), 4.0 * (l1 - l2), 4.0 * (l2 - l3)
                for side in range(2):
                    r = j + 1 + side
                    tm, tp = here * ys[side, c, 3, j + 1], here * ys[side, c, 4, j + 1]
                    slope = (tm - tp) + (
                        before * ys[side, c, 4, j] - after * ys[side, c, 3, j + 2]
                    )
                    gm, gd = cell_adjoint(
                        yc[side, c, 0, r + extra], yc[side, c, 1, r + extra],
                        here * ys[side, c, 1, j + 1], after * ys[side, c, 0, j + 2],
                        before * ys[side, c, 2, j],
                        slope + (1.0 / 24.0) * here, -0.5 * (l2 if side else l1),
                    )
                    pq[side, c, 0, r + 1] = gd + gm
                    pq[side, c, 1, r + 1] = gd - gm

        loop(0, rows + 3, cells)

        def gather(r):
            u = state(u_ref, r + extra)
            ir, v, p = flow(u)
            parts = ([None] * 5, [None] * 5)
            for c in range(count):
                for side in range(2):
                    parts[side][c] = (
                        pq[side, c, 0, r] + pq[side, c, 1, r + 2]
                        - (pq[side, c, 0, r + 1] + pq[side, c, 1, r + 1])
                    )
            grad = [None] * 5
            split_adjoint(u, ir, v, p, 1, parts[0], parts[1], grad)
            for c in range(5):
                gu[c, r] = grad[c]

        def gather_edges(r):
            gather(r)
            gather(r + rows + 3)

        loop(0, 3, gather_edges)
        copies = exchange(
            slot,
            (
                (gu.at[:, pl.ds(0, 3)], rg.at[1]),
                (gu.at[:, pl.ds(rows + 3, 3)], rg.at[0]),
            ),
        )
        loop(3, rows + 3, gather)
        return copies

    def back_local(u_ref, gu, st, pad, count):
        def body(i):
            u = state(u_ref, i + pad)
            ir, v, p = flow(u)
            grad = [gu[c, i + 3] for c in range(5)]
            for number, d, axis in ((0, 0, X_AXIS), (1, 2, Z_AXIS)):
                parts = ([None] * 5, [None] * 5)
                for c in range(count):
                    value = lam[c, i + 3]
                    h4 = 4.0 * (value - nxt(value, axis))
                    for side, h in enumerate((h4, prv(h4, axis))):
                        kept = [st[number, side, c, q, i] for q in range(7)]
                        parts[side][c] = rolled_adjoint(kept, value, h, axis)
                split_adjoint(u, ir, v, p, d, parts[0], parts[1], grad)
            for c in range(5):
                rate[c, i] = grad[c]

        loop(0, rows, body)

    def add_edges(rg):
        def body(i):
            for c in range(5):
                rate[c, i] = rate[c, i] + rg[0, c, i]

        def body_last(i):
            for c in range(5):
                rate[c, i + rows - 3] = rate[c, i + rows - 3] + rg[1, c, i]

        loop(0, 3, body)
        loop(0, 3, body_last)

    copies_g2 = back_y(3, u2, yc2, ys2, gu2, rg2, 5, 4)
    back_local(u2, gu2, st2, 5, 4)
    arrived(copies_g2)
    add_edges(rg2)

    def grad_one(i):
        for c in range(5):
            value = rate[c, i] if c == 4 else 0.25 * two[c, i] + rate[c, i]
            lam[c, i + 3] = DT * value
            two[c, i] = value if c == 4 else 0.75 * two[c, i] + value

    loop(0, rows, grad_one)

    copies_g1 = back_y(4, u1, yc1, ys1, gu1, rg1, 3, 5)
    back_local(u1, gu1, st1, 3, 5)
    arrived(copies_g1)
    add_edges(rg1)

    def finish(i):
        for c in range(5):
            g_ref[strided(c, i), :] = two[c, i] + rate[c, i]

    loop(0, rows, finish)
    for copies in (copies_u, copies_t, copies_2, copies_g2, copies_g1):
        for copy in copies:
            copy.wait_send()


def body(conserved, target):
    rows = conserved.shape[2]
    tile = conserved.shape[1::2]

    def vmem(*lead):
        return pltpu.VMEM(lead + tile, jnp.float32)

    grad, vorticity = pl.pallas_call(
        functools.partial(kernel, rows),
        out_shape=(
            jax.ShapeDtypeStruct((5 * tile[0] * rows, tile[1]), jnp.float32),
            jax.ShapeDtypeStruct((3 * tile[0] * rows, tile[1]), jnp.float32),
        ),
        in_specs=[pl.BlockSpec(memory_space=pltpu.HBM)] * 2,
        out_specs=[pl.BlockSpec(memory_space=pltpu.VMEM)] * 2,
        scratch_shapes=[
            pltpu.VMEM((5 * tile[0] * rows, tile[1]), jnp.float32),
            pltpu.VMEM((3 * tile[0] * rows, tile[1]), jnp.float32),
            vmem(5, rows + 6), vmem(5, rows + 10), vmem(3, rows + 4), vmem(3, rows + 2),
            vmem(3, rows + 2), vmem(5, rows + 4), vmem(5, rows), vmem(rows + 4), vmem(5, rows + 6),
            vmem(2, 5, rows + 6), vmem(2, 5, rows + 10),
            vmem(2, 5, 5, rows + 6), vmem(2, 5, 5, rows + 10),
            vmem(5, rows + 5), vmem(2, 5, 5, rows + 5), vmem(2, 4, 5, rows + 5),
            vmem(2, 2, 5, 7, rows), vmem(2, 2, 4, 7, rows), vmem(2, 5, 2, rows + 8),
            vmem(5, rows + 6), vmem(5, rows + 6), vmem(2, 5, 3), vmem(2, 5, 3),
            pltpu.SemaphoreType.DMA((2,)),
            pltpu.SemaphoreType.DMA((5, 2)),
            pltpu.SemaphoreType.DMA((5, 2)),
        ],
        compiler_params=pltpu.CompilerParams(
            collective_id=0, has_side_effects=True, vmem_limit_bytes=40 * 1024 * 1024
        ),
    )(conserved.reshape(-1, tile[1]), target.reshape(-1, tile[1]))
    return grad.reshape(conserved.shape), vorticity.reshape(target.shape)


def solution(mesh):
    spec = P(None, "run", "gy", None)
    return jax.shard_map(
        body, mesh=mesh, in_specs=(spec, spec), out_specs=(spec, spec), check_vma=False
    )
```

```python
import functools

import jax
import jax.numpy as jnp
from jax import lax
from jax.experimental import pallas as pl
from jax.experimental.pallas import tpu as pltpu
from jax.sharding import PartitionSpec as P

SPEED = 2.5
DT = 0.2
X_AXIS, Z_AXIS = 0, 1
MESH = pl.DeviceIdType.MESH


def inv(x):
    return pltpu.reciprocal(x, approx=True)


def prv(x, axis):
    return pltpu.roll(x, 1, axis)


def nxt(x, axis):
    return pltpu.roll(x, x.shape[axis] - 1, axis)


def flow(u):
    ir = inv(u[0])
    v = [u[k] * ir for k in (1, 2, 3)]
    p = 0.4 * (u[4] - 0.5 * (u[1] * v[0] + u[2] * v[1] + u[3] * v[2]))
    return ir, v, p


def split(u, v, p, d):
    vd = v[d]
    flux = [u[d + 1]]
    for k in range(3):
        term = u[k + 1] * vd
        flux.append(term + p if k == d else term)
    flux.append((u[4] + p) * vd)
    out = []
    for f, q in zip(flux, u):
        half, wave = 0.5 * f, (0.5 * SPEED) * q
        out.append((half + wave, half - wave))
    return out


def split_adjoint(u, ir, v, p, d, gp, gm, grad):
    f = [None if a is None else 0.5 * (a + b) for a, b in zip(gp, gm)]
    for k in range(5):
        if gp[k] is not None:
            grad[k] = plus(grad[k], (0.5 * SPEED) * (gp[k] - gm[k]))
    vd = v[d]
    cp = f[d + 1]
    cv = f[1] * u[1] + f[2] * u[2] + f[3] * u[3]
    if f[4] is not None:
        cp = cp + f[4] * vd
        cv = cv + f[4] * (u[4] + p)
        grad[4] = plus(grad[4], f[4] * vd)
    cp = 0.4 * cp
    grad[4] = plus(grad[4], cp)
    cv = cv * ir
    for k in range(3):
        grad[k + 1] = plus(grad[k + 1], f[k + 1] * vd - v[k] * cp)
    grad[d + 1] = grad[d + 1] + (f[0] + cv)
    speed2 = v[0] * v[0] + v[1] * v[1] + v[2] * v[2]
    grad[0] = plus(grad[0], 0.5 * speed2 * cp - cv * vd)


def plus(a, b):
    return b if a is None else a + b


def cell(um, u, up):
    m = up - um
    d = (up - u) - (u - um)
    e = d + d
    q = (13.0 / 3.0) * (d * d) + 0.4
    a, b = m + e, m - e
    return m, d, q + m * m, q + a * a, q + b * b


LINEAR = ((1.0, 3.0), (3.0, 1.0))
SLOPE = ((1.0 / 3.0, 0.5), (0.5, 1.0 / 3.0))


def correction(bm, bc, bp, tm, tp, side):
    lm, lp = LINEAR[side]
    km, kp = SLOPE[side]
    tau = bm - bp
    rm, rc, rp = inv(bm), inv(bc), inv(bp)
    ym, yc, yp = tau * rm, tau * rc, tau * rp
    zm, zc, zp = ym * ym, yc * yc, yp * yp
    am, ap = 1.0 + zm, 1.0 + zp
    ktm, ktp = km * tm, kp * tp
    rt = inv((10.0 + lm * zm) + (6.0 * zc + lp * zp))
    value = (am * ktm + ap * ktp) * rt
    dm = (ktm - lm * value) * (ym * rm)
    dc = (-6.0 * value) * (yc * rc)
    dp = (ktp - lp * value) * (yp * rp)
    sk = dm + dc + dp
    return value, (
        sk - dm * ym, dc * yc, sk + dp * yp, (0.25 * km) * am, (0.25 * kp) * ap, rt if side == 0 else -rt
    )


def cell_adjoint(m, d, gc, gr, gl, d_extra, m_extra):
    both = gr - gl
    total = both - gc
    delta = 2.0 * (gr + gl)
    gm = total * m + delta * d + m_extra
    gd = ((13.0 / 3.0) * total + 4.0 * both) * d + delta * m + d_extra
    return gm, gd


def rolled_term(f, axis, side, keep):
    m, d, bc, br, bl = cell(prv(f, axis), f, nxt(f, axis))
    tp = nxt(d, axis) - d
    r, coefs = correction(prv(br, axis), bc, nxt(bl, axis), prv(tp, axis), tp, side)
    if keep is not None:
        keep((m, d) + coefs)
    if side == 0:
        a = (1.0 / 6.0) * d + r
        return a - prv(a, axis) - 0.5 * m
    a = (1.0 / 6.0) * d - r
    return nxt(a, axis) - a - 0.5 * m


def rolled_adjoint(kept, lam, h4, axis):
    m, d, cbm, cbc, cbp, ctm, ctp, factor = kept
    hs = h4 * factor
    w = hs * ctp + nxt(hs * ctm, axis)
    extra = (1.0 / 24.0) * h4 + (prv(w, axis) - w)
    gm, gd = cell_adjoint(
        m, d, hs * cbc, nxt(hs * cbm, axis), prv(hs * cbp, axis), extra, -0.5 * lam
    )
    return prv(gd + gm, axis) + nxt(gd - gm, axis) - 2.0 * gd


def central(x, axis):
    return 0.5 * (nxt(x, axis) - prv(x, axis))


def kernel(
    rows, c_any, t_any, g_ref, o_ref,
    c_ref, t_ref, u1, u2, wv, tg, res, rate, two, ivs, lam, f1, f2, yc1, yc2, za, ys1, ys2,
    st1, st2, pq, gu1, gu2, rg1, rg2, local, send, recv,
):
    loads = [
        pltpu.make_async_copy(c_any, c_ref, local.at[0]),
        pltpu.make_async_copy(t_any, t_ref, local.at[1]),
    ]
    for load in loads:
        load.start()
    size = lax.axis_size("gy")
    me = lax.axis_index("gy")
    right, left = lax.rem(me + 1, size), lax.rem(me + size - 1, size)
    barrier = pltpu.get_barrier_semaphore()
    for other in (left, right):
        pl.semaphore_signal(barrier, inc=1, device_id={"gy": other}, device_id_type=MESH)

    def loop(low, high, body):
        lax.fori_loop(low, high, lambda i, _: (body(i), 0)[1], 0)

    def each_row(body):
        step = 2 if rows % 2 == 0 else 1
        loop(0, rows // step, lambda i: [body(step * i + n) for n in range(step)])

    def exchange(slot, pairs):
        copies = []
        for side, (other, (src, dst)) in enumerate(zip((left, right), pairs)):
            copies.append(
                pltpu.make_async_remote_copy(
                    src_ref=src, dst_ref=dst,
                    send_sem=send.at[slot, side], recv_sem=recv.at[slot, side],
                    device_id={"gy": other}, device_id_type=MESH,
                )
            )
        for copy in copies:
            copy.start()
        return copies

    def halo(slot, ref, width):
        return exchange(
            slot,
            (
                (ref.at[:, pl.ds(width, width)], ref.at[:, pl.ds(width + rows, width)]),
                (ref.at[:, pl.ds(rows, width)], ref.at[:, pl.ds(0, width)]),
            ),
        )

    def arrived(copies):
        for copy in copies:
            copy.wait_recv()

    def strided(component, row):
        return pl.ds(component * (8 * rows) + row, 8, stride=rows)

    def load_row(i):
        for c in range(5):
            u1[c, i + 3] = c_ref[strided(c, i), :]
        for c in range(3):
            tg[c, i + 1] = t_ref[strided(c, i), :]

    zero = jnp.zeros((8, 128), jnp.float32)

    for load in loads:
        load.wait()
    loop(0, rows, load_row)
    pl.semaphore_wait(barrier, 2)
    copies_u = halo(0, u1, 3)
    copies_t = halo(1, tg, 1)

    def clear(i):
        for side in range(2):
            for c in range(5):
                for q in range(6):
                    ys1[side, c, q, i] = zero
                    ys1[side, c, q, i + rows + 3] = zero

    loop(0, 2, clear)

    def clear_pq(i):
        for side in range(2):
            for c in range(5):
                for q in range(2):
                    pq[side, c, q, i] = zero
                    pq[side, c, q, i + rows + 5] = zero

    loop(0, 3, clear_pq)

    def clear_lam(i):
        for c in range(5):
            lam[c, i] = zero
            lam[c, i + rows + 3] = zero

    loop(0, 3, clear_lam)

    def state(ref, row):
        return [ref[c, row] for c in range(5)]

    def flux_y(u_ref, f_ref, row):
        u = state(u_ref, row)
        _, v, p = flow(u)
        for c, pair in enumerate(split(u, v, p, 1)):
            f_ref[0, c, row] = pair[0]
            f_ref[1, c, row] = pair[1]

    def row_rate(u_ref, f_ref, st, pad, count, i):
        u = state(u_ref, i + pad)
        _, v, p = flow(u)
        if st is not None:
            for c, pair in enumerate(split(u, v, p, 1)):
                f_ref[0, c, i + pad] = pair[0]
                f_ref[1, c, i + pad] = pair[1]
        fx = split(u, v, p, 0)
        fz = split(u, v, p, 2)
        for c in range(count):
            total = None
            for side in range(2):
                for number, f, axis in ((0, fx, X_AXIS), (1, fz, Z_AXIS)):

                    def keep(values):
                        for q, value in enumerate(values):
                            st[number, side, c, q, i] = value

                    use = keep if st is not None else None
                    total = plus(total, rolled_term(f[c][side], axis, side, use))
            rate[c, i + pad - 3] = total

    def rate_y(u_ref, f_ref, yc, ys, pad, count):
        extra = pad - 3

        def edges(i):
            flux_y(u_ref, f_ref, i)
            flux_y(u_ref, f_ref, i + rows + pad)

        loop(0, pad, edges)

        def cells(i):
            for c in range(count):
                for side in range(2):
                    r = i + 1
                    values = cell(f_ref[side, c, r - 1], f_ref[side, c, r], f_ref[side, c, r + 1])
                    for q in range(5):
                        yc[side, c, q, r] = values[q]

        loop(0, rows + 2 * pad - 2, cells)

        def faces(k):
            for c in range(count):
                total = None
                for side in range(2):
                    r = k + 2 + side
                    d = yc[side, c, 1, r]
                    x, coefs = correction(
                        yc[side, c, 3, r - 1], yc[side, c, 2, r], yc[side, c, 4, r + 1],
                        d - yc[side, c, 1, r - 1], yc[side, c, 1, r + 1] - d, side,
                    )
                    for q, value in enumerate(coefs):
                        ys[side, c, q, k + 2 - extra] = value
                    a = (1.0 / 6.0) * d
                    total = plus(total, a + x if side == 0 else a - x)
                za[c, k] = total

        loop(0, rows + 1 + 2 * extra, faces)

    def whole_rate(yc, c, i):
        return rate[c, i] + (
            (za[c, i + 1] - za[c, i]) - 0.5 * (yc[0, c, 0, i + 3] + yc[1, c, 0, i + 3])
        )

    each_row(lambda i: row_rate(u1, f1, st1, 3, 5, i))
    arrived(copies_u)
    rate_y(u1, f1, yc1, ys1, 3, 5)

    def first(i):
        for c in range(5):
            u2[c, i + 5] = u1[c, i + 3] + DT * whole_rate(yc1, c, i)

    loop(0, rows, first)
    copies_2 = halo(2, u2, 5)

    each_row(lambda i: row_rate(u2, f2, st2, 5, 4, i))
    arrived(copies_2)

    def beside(i):
        row_rate(u2, f2, None, 5, 4, i - 2)
        row_rate(u2, f2, None, 5, 4, i + rows)

    loop(0, 2, beside)
    rate_y(u2, f2, yc2, ys2, 5, 4)

    def second(i):
        s = []
        for c in range(4):
            s.append(
                0.75 * u1[c, i + 1] + 0.25 * (u2[c, i + 3] + DT * whole_rate(yc2, c, i))
            )
        ir = inv(s[0])
        ivs[i] = ir
        for k in range(3):
            wv[k, i] = s[k + 1] * ir

    loop(0, rows + 4, second)
    arrived(copies_t)

    def curl(i):
        x, y, z = wv[0, i + 1], wv[1, i + 1], wv[2, i + 1]
        vort = (
            0.5 * (wv[2, i + 2] - wv[2, i]) - central(y, Z_AXIS),
            central(x, Z_AXIS) - central(z, X_AXIS),
            central(y, X_AXIS) - 0.5 * (wv[0, i + 2] - wv[0, i]),
        )
        for k in range(3):
            res[k, i] = vort[k] - tg[k, i]
        return vort

    def curl_own(i):
        vort = curl(i + 1)
        for k in range(3):
            o_ref[strided(k, i), :] = vort[k]

    loop(0, rows, curl_own)
    curl(0)
    curl(rows + 1)

    def back_two(i):
        a, b, c = res[0, i + 1], res[1, i + 1], res[2, i + 1]
        gw = (
            0.5 * (res[2, i + 2] - res[2, i]) - central(b, Z_AXIS),
            central(a, Z_AXIS) - central(c, X_AXIS),
            central(b, X_AXIS) - 0.5 * (res[0, i + 2] - res[0, i]),
        )
        ir = ivs[i + 2]
        gw = [ir * g for g in gw]
        grad = [-(gw[0] * wv[0, i + 2] + gw[1] * wv[1, i + 2] + gw[2] * wv[2, i + 2])] + gw
        for c in range(4):
            two[c, i] = grad[c]
            lam[c, i + 3] = (0.25 * DT) * grad[c]

    loop(0, rows, back_two)

    def back_y(slot, u_ref, yc, ys, gu, rg, pad, count):
        extra = pad - 3

        def cells(j):
            for c in range(count):
                l0, l1, l2, l3 = (lam[c, j + n] for n in range(4))
                before, here, after = 4.0 * (l0 - l1), 4.0 * (l1 - l2), 4.0 * (l2 - l3)
                for side in range(2):
                    r = j + 1 + side
                    b, h, a = (
                        x * ys[side, c, 5, j + n] for n, x in enumerate((before, here, after))
                    )
                    slope = h * (ys[side, c, 3, j + 1] - ys[side, c, 4, j + 1]) + (
                        b * ys[side, c, 4, j] - a * ys[side, c, 3, j + 2]
                    )
                    gm, gd = cell_adjoint(
                        yc[side, c, 0, r + extra], yc[side, c, 1, r + extra],
                        h * ys[side, c, 1, j + 1], a * ys[side, c, 0, j + 2],
                        b * ys[side, c, 2, j],
                        slope + (1.0 / 24.0) * here, -0.5 * (l2 if side else l1),
                    )
                    pq[side, c, 0, r + 1] = gd + gm
                    pq[side, c, 1, r + 1] = gd - gm

        loop(0, rows + 3, cells)

        def gather(r):
            u = state(u_ref, r + extra)
            ir, v, p = flow(u)
            parts = ([None] * 5, [None] * 5)
            for c in range(count):
                for side in range(2):
                    parts[side][c] = (
                        pq[side, c, 0, r] + pq[side, c, 1, r + 2]
                        - (pq[side, c, 0, r + 1] + pq[side, c, 1, r + 1])
                    )
            grad = [None] * 5
            split_adjoint(u, ir, v, p, 1, parts[0], parts[1], grad)
            for c in range(5):
                gu[c, r] = grad[c]

        def gather_edges(r):
            gather(r)
            gather(r + rows + 3)

        loop(0, 3, gather_edges)
        copies = exchange(
            slot,
            (
                (gu.at[:, pl.ds(0, 3)], rg.at[1]),
                (gu.at[:, pl.ds(rows + 3, 3)], rg.at[0]),
            ),
        )
        loop(3, rows + 3, gather)
        return copies

    def back_local(u_ref, gu, st, pad, count):
        def body(i):
            u = state(u_ref, i + pad)
            ir, v, p = flow(u)
            grad = [gu[c, i + 3] for c in range(5)]
            for number, d, axis in ((0, 0, X_AXIS), (1, 2, Z_AXIS)):
                parts = ([None] * 5, [None] * 5)
                for c in range(count):
                    value = lam[c, i + 3]
                    h4 = 4.0 * (value - nxt(value, axis))
                    for side, h in enumerate((h4, prv(h4, axis))):
                        kept = [st[number, side, c, q, i] for q in range(8)]
                        parts[side][c] = rolled_adjoint(kept, value, h, axis)
                split_adjoint(u, ir, v, p, d, parts[0], parts[1], grad)
            for c in range(5):
                rate[c, i] = grad[c]

        each_row(body)

    def add_edges(rg):
        def body(i):
            for c in range(5):
                rate[c, i] = rate[c, i] + rg[0, c, i]

        def body_last(i):
            for c in range(5):
                rate[c, i + rows - 3] = rate[c, i + rows - 3] + rg[1, c, i]

        loop(0, 3, body)
        loop(0, 3, body_last)

    copies_g2 = back_y(3, u2, yc2, ys2, gu2, rg2, 5, 4)
    back_local(u2, gu2, st2, 5, 4)
    arrived(copies_g2)
    add_edges(rg2)

    def grad_one(i):
        for c in range(5):
            value = rate[c, i] if c == 4 else 0.25 * two[c, i] + rate[c, i]
            lam[c, i + 3] = DT * value
            two[c, i] = value if c == 4 else 0.75 * two[c, i] + value

    loop(0, rows, grad_one)

    copies_g1 = back_y(4, u1, yc1, ys1, gu1, rg1, 3, 5)
    back_local(u1, gu1, st1, 3, 5)
    arrived(copies_g1)
    add_edges(rg1)

    def finish(i):
        for c in range(5):
            g_ref[strided(c, i), :] = two[c, i] + rate[c, i]

    loop(0, rows, finish)
    for copies in (copies_u, copies_t, copies_2, copies_g2, copies_g1):
        for copy in copies:
            copy.wait_send()


def body(conserved, target):
    rows = conserved.shape[2]
    tile = conserved.shape[1::2]

    def vmem(*lead):
        return pltpu.VMEM(lead + tile, jnp.float32)

    grad, vorticity = pl.pallas_call(
        functools.partial(kernel, rows),
        out_shape=(
            jax.ShapeDtypeStruct((5 * tile[0] * rows, tile[1]), jnp.float32),
            jax.ShapeDtypeStruct((3 * tile[0] * rows, tile[1]), jnp.float32),
        ),
        in_specs=[pl.BlockSpec(memory_space=pltpu.HBM)] * 2,
        out_specs=[pl.BlockSpec(memory_space=pltpu.VMEM)] * 2,
        scratch_shapes=[
            pltpu.VMEM((5 * tile[0] * rows, tile[1]), jnp.float32),
            pltpu.VMEM((3 * tile[0] * rows, tile[1]), jnp.float32),
            vmem(5, rows + 6), vmem(5, rows + 10), vmem(3, rows + 4), vmem(3, rows + 2),
            vmem(3, rows + 2), vmem(5, rows + 4), vmem(5, rows), vmem(rows + 4), vmem(5, rows + 6),
            vmem(2, 5, rows + 6), vmem(2, 5, rows + 10),
            vmem(2, 5, 5, rows + 6), vmem(2, 5, 5, rows + 10),
            vmem(5, rows + 5), vmem(2, 5, 6, rows + 5), vmem(2, 4, 6, rows + 5),
            vmem(2, 2, 5, 8, rows), vmem(2, 2, 4, 8, rows), vmem(2, 5, 2, rows + 8),
            vmem(5, rows + 6), vmem(5, rows + 6), vmem(2, 5, 3), vmem(2, 5, 3),
            pltpu.SemaphoreType.DMA((2,)),
            pltpu.SemaphoreType.DMA((5, 2)),
            pltpu.SemaphoreType.DMA((5, 2)),
        ],
        compiler_params=pltpu.CompilerParams(
            collective_id=0, has_side_effects=True, vmem_limit_bytes=40 * 1024 * 1024
        ),
    )(conserved.reshape(-1, tile[1]), target.reshape(-1, tile[1]))
    return grad.reshape(conserved.shape), vorticity.reshape(target.shape)


def solution(mesh):
    spec = P(None, "run", "gy", None)
    return jax.shard_map(
        body, mesh=mesh, in_specs=(spec, spec), out_specs=(spec, spec), check_vma=False
    )
```

```python
import functools

import jax
import jax.numpy as jnp
from jax import lax
from jax.experimental import pallas as pl
from jax.experimental.pallas import tpu as pltpu
from jax.sharding import PartitionSpec as P

SPEED = 2.5
DT = 0.2
X_AXIS, Z_AXIS = 0, 1
MESH = pl.DeviceIdType.MESH


def inv(x):
    return pltpu.reciprocal(x, approx=True)


def prv(x, axis):
    return pltpu.roll(x, 1, axis)


def nxt(x, axis):
    return pltpu.roll(x, x.shape[axis] - 1, axis)


def flow(u):
    ir = inv(u[0])
    v = [u[k] * ir for k in (1, 2, 3)]
    p = 0.4 * (u[4] - 0.5 * (u[1] * v[0] + u[2] * v[1] + u[3] * v[2]))
    return ir, v, p


def split(u, v, p, d):
    vd = v[d]
    flux = [u[d + 1]]
    for k in range(3):
        term = u[k + 1] * vd
        flux.append(term + p if k == d else term)
    flux.append((u[4] + p) * vd)
    out = []
    for f, q in zip(flux, u):
        half, wave = 0.5 * f, (0.5 * SPEED) * q
        out.append((half + wave, half - wave))
    return out


def split_adjoint(u, ir, v, p, d, gp, gm, grad):
    f = [None if a is None else 0.5 * (a + b) for a, b in zip(gp, gm)]
    for k in range(5):
        if gp[k] is not None:
            grad[k] = plus(grad[k], (0.5 * SPEED) * (gp[k] - gm[k]))
    vd = v[d]
    cp = f[d + 1]
    cv = f[1] * u[1] + f[2] * u[2] + f[3] * u[3]
    if f[4] is not None:
        cp = cp + f[4] * vd
        cv = cv + f[4] * (u[4] + p)
        grad[4] = plus(grad[4], f[4] * vd)
    cp = 0.4 * cp
    grad[4] = plus(grad[4], cp)
    cv = cv * ir
    for k in range(3):
        grad[k + 1] = plus(grad[k + 1], f[k + 1] * vd - v[k] * cp)
    grad[d + 1] = grad[d + 1] + (f[0] + cv)
    speed2 = v[0] * v[0] + v[1] * v[1] + v[2] * v[2]
    grad[0] = plus(grad[0], 0.5 * speed2 * cp - cv * vd)


def plus(a, b):
    return b if a is None else a + b


def cell(um, u, up):
    m = up - um
    d = (up - u) - (u - um)
    e = d + d
    q = (13.0 / 3.0) * (d * d) + 0.4
    a, b = m + e, m - e
    return m, d, q + m * m, q + a * a, q + b * b


LINEAR = ((1.0, 3.0), (3.0, 1.0))
SLOPE = ((1.0 / 3.0, 0.5), (0.5, 1.0 / 3.0))


def correction(bm, bc, bp, tm, tp, side):
    lm, lp = LINEAR[side]
    km, kp = SLOPE[side]
    tau = bm - bp
    rm, rc, rp = inv(bm), inv(bc), inv(bp)
    ym, yc, yp = tau * rm, tau * rc, tau * rp
    zm, zc, zp = ym * ym, yc * yc, yp * yp
    am, ap = 1.0 + zm, 1.0 + zp
    ktm, ktp = km * tm, kp * tp
    rt = inv((10.0 + lm * zm) + (6.0 * zc + lp * zp))
    value = (am * ktm + ap * ktp) * rt
    dm = (ktm - lm * value) * (ym * rm)
    dc = (-6.0 * value) * (yc * rc)
    dp = (ktp - lp * value) * (yp * rp)
    sk = dm + dc + dp
    return value, (
        sk - dm * ym, dc * yc, sk + dp * yp, (0.25 * km) * am, (0.25 * kp) * ap, rt if side == 0 else -rt
    )


def cell_adjoint(m, d, gc, gr, gl, d_extra, m_extra):
    both = gr - gl
    total = both - gc
    delta = 2.0 * (gr + gl)
    gm = total * m + delta * d + m_extra
    gd = ((13.0 / 3.0) * total + 4.0 * both) * d + delta * m + d_extra
    return gm, gd


def rolled_term(f, axis, side, keep):
    m, d, bc, br, bl = cell(prv(f, axis), f, nxt(f, axis))
    tp = nxt(d, axis) - d
    r, coefs = correction(prv(br, axis), bc, nxt(bl, axis), prv(tp, axis), tp, side)
    if keep is not None:
        keep((m, d) + coefs)
    if side == 0:
        a = (1.0 / 6.0) * d + r
        return a - prv(a, axis) - 0.5 * m
    a = (1.0 / 6.0) * d - r
    return nxt(a, axis) - a - 0.5 * m


def rolled_adjoint(kept, lam, h4, axis):
    m, d, cbm, cbc, cbp, ctm, ctp, factor = kept
    hs = h4 * factor
    w = hs * ctp + nxt(hs * ctm, axis)
    extra = (1.0 / 24.0) * h4 + (prv(w, axis) - w)
    gm, gd = cell_adjoint(
        m, d, hs * cbc, nxt(hs * cbm, axis), prv(hs * cbp, axis), extra, -0.5 * lam
    )
    return prv(gd + gm, axis) + nxt(gd - gm, axis) - 2.0 * gd


def central(x, axis):
    return 0.5 * (nxt(x, axis) - prv(x, axis))


def kernel(
    rows, c_ref, t_ref, g_ref, o_ref,
    u1, u2, wv, tg, res, rate, two, ivs, lam, f1, f2, yc1, yc2, za, ys1, ys2,
    st1, st2, pq, gu1, gu2, rg1, rg2, send, recv,
):
    size = lax.axis_size("gy")
    me = lax.axis_index("gy")
    right, left = lax.rem(me + 1, size), lax.rem(me + size - 1, size)
    barrier = pltpu.get_barrier_semaphore()
    for other in (left, right):
        pl.semaphore_signal(barrier, inc=1, device_id={"gy": other}, device_id_type=MESH)

    def loop(low, high, body):
        lax.fori_loop(low, high, lambda i, _: (body(i), 0)[1], 0)

    def each_row(body):
        step = 2 if rows % 2 == 0 else 1
        loop(0, rows // step, lambda i: [body(step * i + n) for n in range(step)])

    def exchange(slot, pairs):
        copies = []
        for side, (other, (src, dst)) in enumerate(zip((left, right), pairs)):
            copies.append(
                pltpu.make_async_remote_copy(
                    src_ref=src, dst_ref=dst,
                    send_sem=send.at[slot, side], recv_sem=recv.at[slot, side],
                    device_id={"gy": other}, device_id_type=MESH,
                )
            )
        for copy in copies:
            copy.start()
        return copies

    def halo(slot, ref, width):
        return exchange(
            slot,
            (
                (ref.at[:, pl.ds(width, width)], ref.at[:, pl.ds(width + rows, width)]),
                (ref.at[:, pl.ds(rows, width)], ref.at[:, pl.ds(0, width)]),
            ),
        )

    def arrived(copies):
        for copy in copies:
            copy.wait_recv()

    def strided(component, row):
        return pl.ds(component * (8 * rows) + row, 8, stride=rows)

    def load_row(i):
        for c in range(5):
            u1[c, i + 3] = c_ref[strided(c, i), :]
        for c in range(3):
            tg[c, i + 1] = t_ref[strided(c, i), :]

    zero = jnp.zeros((8, 128), jnp.float32)

    loop(0, rows, load_row)
    pl.semaphore_wait(barrier, 2)
    copies_u = halo(0, u1, 3)
    copies_t = halo(1, tg, 1)

    def clear(i):
        for side in range(2):
            for c in range(5):
                for q in range(6):
                    ys1[side, c, q, i] = zero
                    ys1[side, c, q, i + rows + 3] = zero

    loop(0, 2, clear)

    def clear_pq(i):
        for side in range(2):
            for c in range(5):
                for q in range(2):
                    pq[side, c, q, i] = zero
                    pq[side, c, q, i + rows + 5] = zero

    loop(0, 3, clear_pq)

    def clear_lam(i):
        for c in range(5):
            lam[c, i] = zero
            lam[c, i + rows + 3] = zero

    loop(0, 3, clear_lam)

    def state(ref, row):
        return [ref[c, row] for c in range(5)]

    def flux_y(u_ref, f_ref, row):
        u = state(u_ref, row)
        _, v, p = flow(u)
        for c, pair in enumerate(split(u, v, p, 1)):
            f_ref[0, c, row] = pair[0]
            f_ref[1, c, row] = pair[1]

    def row_rate(u_ref, f_ref, st, pad, count, i):
        u = state(u_ref, i + pad)
        _, v, p = flow(u)
        if st is not None:
            for c, pair in enumerate(split(u, v, p, 1)):
                f_ref[0, c, i + pad] = pair[0]
                f_ref[1, c, i + pad] = pair[1]
        fx = split(u, v, p, 0)
        fz = split(u, v, p, 2)
        for c in range(count):
            total = None
            for side in range(2):
                for number, f, axis in ((0, fx, X_AXIS), (1, fz, Z_AXIS)):

                    def keep(values):
                        for q, value in enumerate(values):
                            st[number, side, c, q, i] = value

                    use = keep if st is not None else None
                    total = plus(total, rolled_term(f[c][side], axis, side, use))
            rate[c, i + pad - 3] = total

    def rate_y(u_ref, f_ref, yc, ys, pad, count):
        extra = pad - 3

        def edges(i):
            flux_y(u_ref, f_ref, i)
            flux_y(u_ref, f_ref, i + rows + pad)

        loop(0, pad, edges)

        def cells(i):
            for c in range(count):
                for side in range(2):
                    r = i + 1
                    values = cell(f_ref[side, c, r - 1], f_ref[side, c, r], f_ref[side, c, r + 1])
                    for q in range(5):
                        yc[side, c, q, r] = values[q]

        loop(0, rows + 2 * pad - 2, cells)

        def faces(k):
            for c in range(count):
                total = None
                for side in range(2):
                    r = k + 2 + side
                    d = yc[side, c, 1, r]
                    x, coefs = correction(
                        yc[side, c, 3, r - 1], yc[side, c, 2, r], yc[side, c, 4, r + 1],
                        d - yc[side, c, 1, r - 1], yc[side, c, 1, r + 1] - d, side,
                    )
                    for q, value in enumerate(coefs):
                        ys[side, c, q, k + 2 - extra] = value
                    a = (1.0 / 6.0) * d
                    total = plus(total, a + x if side == 0 else a - x)
                za[c, k] = total

        loop(0, rows + 1 + 2 * extra, faces)

    def whole_rate(yc, c, i):
        return rate[c, i] + (
            (za[c, i + 1] - za[c, i]) - 0.5 * (yc[0, c, 0, i + 3] + yc[1, c, 0, i + 3])
        )

    each_row(lambda i: row_rate(u1, f1, st1, 3, 5, i))
    arrived(copies_u)
    rate_y(u1, f1, yc1, ys1, 3, 5)

    def first(i):
        for c in range(5):
            u2[c, i + 5] = u1[c, i + 3] + DT * whole_rate(yc1, c, i)

    loop(0, rows, first)
    copies_2 = halo(2, u2, 5)

    each_row(lambda i: row_rate(u2, f2, st2, 5, 4, i))
    arrived(copies_2)

    def beside(i):
        row_rate(u2, f2, None, 5, 4, i - 2)
        row_rate(u2, f2, None, 5, 4, i + rows)

    loop(0, 2, beside)
    rate_y(u2, f2, yc2, ys2, 5, 4)

    def second(i):
        s = []
        for c in range(4):
            s.append(
                0.75 * u1[c, i + 1] + 0.25 * (u2[c, i + 3] + DT * whole_rate(yc2, c, i))
            )
        ir = inv(s[0])
        ivs[i] = ir
        for k in range(3):
            wv[k, i] = s[k + 1] * ir

    loop(0, rows + 4, second)
    arrived(copies_t)

    def curl(i):
        x, y, z = wv[0, i + 1], wv[1, i + 1], wv[2, i + 1]
        vort = (
            0.5 * (wv[2, i + 2] - wv[2, i]) - central(y, Z_AXIS),
            central(x, Z_AXIS) - central(z, X_AXIS),
            central(y, X_AXIS) - 0.5 * (wv[0, i + 2] - wv[0, i]),
        )
        for k in range(3):
            res[k, i] = vort[k] - tg[k, i]
        return vort

    def curl_own(i):
        vort = curl(i + 1)
        for k in range(3):
            o_ref[strided(k, i), :] = vort[k]

    loop(0, rows, curl_own)
    curl(0)
    curl(rows + 1)

    def back_two(i):
        a, b, c = res[0, i + 1], res[1, i + 1], res[2, i + 1]
        gw = (
            0.5 * (res[2, i + 2] - res[2, i]) - central(b, Z_AXIS),
            central(a, Z_AXIS) - central(c, X_AXIS),
            central(b, X_AXIS) - 0.5 * (res[0, i + 2] - res[0, i]),
        )
        ir = ivs[i + 2]
        gw = [ir * g for g in gw]
        grad = [-(gw[0] * wv[0, i + 2] + gw[1] * wv[1, i + 2] + gw[2] * wv[2, i + 2])] + gw
        for c in range(4):
            two[c, i] = grad[c]
            lam[c, i + 3] = (0.25 * DT) * grad[c]

    loop(0, rows, back_two)

    def back_y(slot, u_ref, yc, ys, gu, rg, pad, count):
        extra = pad - 3

        def cells(j):
            for c in range(count):
                l0, l1, l2, l3 = (lam[c, j + n] for n in range(4))
                before, here, after = 4.0 * (l0 - l1), 4.0 * (l1 - l2), 4.0 * (l2 - l3)
                for side in range(2):
                    r = j + 1 + side
                    b, h, a = (
                        x * ys[side, c, 5, j + n] for n, x in enumerate((before, here, after))
                    )
                    slope = h * (ys[side, c, 3, j + 1] - ys[side, c, 4, j + 1]) + (
                        b * ys[side, c, 4, j] - a * ys[side, c, 3, j + 2]
                    )
                    gm, gd = cell_adjoint(
                        yc[side, c, 0, r + extra], yc[side, c, 1, r + extra],
                        h * ys[side, c, 1, j + 1], a * ys[side, c, 0, j + 2],
                        b * ys[side, c, 2, j],
                        slope + (1.0 / 24.0) * here, -0.5 * (l2 if side else l1),
                    )
                    pq[side, c, 0, r + 1] = gd + gm
                    pq[side, c, 1, r + 1] = gd - gm

        def cells_edges(j):
            cells(j)
            cells(j + rows)

        loop(0, 3, cells_edges)

        def gather(r):
            u = state(u_ref, r + extra)
            ir, v, p = flow(u)
            parts = ([None] * 5, [None] * 5)
            for c in range(count):
                for side in range(2):
                    parts[side][c] = (
                        pq[side, c, 0, r] + pq[side, c, 1, r + 2]
                        - (pq[side, c, 0, r + 1] + pq[side, c, 1, r + 1])
                    )
            grad = [None] * 5
            split_adjoint(u, ir, v, p, 1, parts[0], parts[1], grad)
            for c in range(5):
                gu[c, r] = grad[c]

        def gather_edges(r):
            gather(r)
            gather(r + rows + 3)

        loop(0, 3, gather_edges)
        copies = exchange(
            slot,
            (
                (gu.at[:, pl.ds(0, 3)], rg.at[1]),
                (gu.at[:, pl.ds(rows + 3, 3)], rg.at[0]),
            ),
        )
        loop(3, rows, cells)
        loop(3, rows + 3, gather)
        return copies

    def back_local(u_ref, gu, st, pad, count):
        def body(i):
            u = state(u_ref, i + pad)
            ir, v, p = flow(u)
            grad = [gu[c, i + 3] for c in range(5)]
            for number, d, axis in ((0, 0, X_AXIS), (1, 2, Z_AXIS)):
                parts = ([None] * 5, [None] * 5)
                for c in range(count):
                    value = lam[c, i + 3]
                    h4 = 4.0 * (value - nxt(value, axis))
                    for side, h in enumerate((h4, prv(h4, axis))):
                        kept = [st[number, side, c, q, i] for q in range(8)]
                        parts[side][c] = rolled_adjoint(kept, value, h, axis)
                split_adjoint(u, ir, v, p, d, parts[0], parts[1], grad)
            for c in range(5):
                rate[c, i] = grad[c]

        each_row(body)

    def add_edges(rg):
        def body(i):
            for c in range(5):
                rate[c, i] = rate[c, i] + rg[0, c, i]

        def body_last(i):
            for c in range(5):
                rate[c, i + rows - 3] = rate[c, i + rows - 3] + rg[1, c, i]

        loop(0, 3, body)
        loop(0, 3, body_last)

    copies_g2 = back_y(3, u2, yc2, ys2, gu2, rg2, 5, 4)
    back_local(u2, gu2, st2, 5, 4)
    arrived(copies_g2)
    add_edges(rg2)

    def grad_one(i):
        for c in range(5):
            value = rate[c, i] if c == 4 else 0.25 * two[c, i] + rate[c, i]
            lam[c, i + 3] = DT * value
            two[c, i] = value if c == 4 else 0.75 * two[c, i] + value

    loop(0, rows, grad_one)

    copies_g1 = back_y(4, u1, yc1, ys1, gu1, rg1, 3, 5)
    back_local(u1, gu1, st1, 3, 5)
    arrived(copies_g1)
    add_edges(rg1)

    def finish(i):
        for c in range(5):
            g_ref[strided(c, i), :] = two[c, i] + rate[c, i]

    loop(0, rows, finish)
    for copies in (copies_u, copies_t, copies_2, copies_g2, copies_g1):
        for copy in copies:
            copy.wait_send()


def body(conserved, target):
    rows = conserved.shape[2]
    tile = conserved.shape[1::2]

    def vmem(*lead):
        return pltpu.VMEM(lead + tile, jnp.float32)

    grad, vorticity = pl.pallas_call(
        functools.partial(kernel, rows),
        out_shape=(
            jax.ShapeDtypeStruct((5 * tile[0] * rows, tile[1]), jnp.float32),
            jax.ShapeDtypeStruct((3 * tile[0] * rows, tile[1]), jnp.float32),
        ),
        in_specs=[pl.BlockSpec(memory_space=pltpu.VMEM)] * 2,
        out_specs=[pl.BlockSpec(memory_space=pltpu.VMEM)] * 2,
        scratch_shapes=[
            vmem(5, rows + 6), vmem(5, rows + 10), vmem(3, rows + 4), vmem(3, rows + 2),
            vmem(3, rows + 2), vmem(5, rows + 4), vmem(5, rows), vmem(rows + 4), vmem(5, rows + 6),
            vmem(2, 5, rows + 6), vmem(2, 5, rows + 10),
            vmem(2, 5, 5, rows + 6), vmem(2, 5, 5, rows + 10),
            vmem(5, rows + 5), vmem(2, 5, 6, rows + 5), vmem(2, 4, 6, rows + 5),
            vmem(2, 2, 5, 8, rows), vmem(2, 2, 4, 8, rows), vmem(2, 5, 2, rows + 8),
            vmem(5, rows + 6), vmem(5, rows + 6), vmem(2, 5, 3), vmem(2, 5, 3),
            pltpu.SemaphoreType.DMA((5, 2)),
            pltpu.SemaphoreType.DMA((5, 2)),
        ],
        compiler_params=pltpu.CompilerParams(
            collective_id=0, has_side_effects=True, vmem_limit_bytes=40 * 1024 * 1024
        ),
    )(conserved.reshape(-1, tile[1]), target.reshape(-1, tile[1]))
    return grad.reshape(conserved.shape), vorticity.reshape(target.shape)


def solution(mesh):
    spec = P(None, "run", "gy", None)
    return jax.shard_map(
        body, mesh=mesh, in_specs=(spec, spec), out_specs=(spec, spec), check_vma=False
    )
```
